1024 devices in a mesh: row: 32 (over y_lo, x, core), col: 32 (over y_hi, z).
Axes of the slice: x: 4, y: 8 (y_hi: 2, y_lo: 4; y = y_hi * 4 + y_lo), z: 16, core: 2. Of those that a mesh axis runs over, the one named last changes fastest.
Arguments:
- left_term: bfloat16 [32, 32, 1, 2, 128, 128], P('row', 'col'), may hold values from -6 to 6
- right_factor: bfloat16 [32, 32, 128, 256], P('row', 'col'), may hold values from -0.75 to 0.75
- targets: int32 [32, 32, 32, 1], P('row', 'col'), may hold values from 0 to 8, as said below
- propagator_in: float32 [32, 32, 8, 2, 128, 128], P('row', 'col'), may hold values from -6 to 6
Outputs:
- next_term: bfloat16 [32, 32, 8, 2, 128, 128], P('row', 'col')
- propagator: float32 [32, 32, 8, 2, 128, 128], P('row', 'col')
The draws below stay inside these ranges and needn't reach their ends.
Inputs may be any that keep to these rules, and one draw needn't show every extreme that they name: `targets`: an entry equal to 8 means the block product is filtered out. On each device the share of entries below 8 is exactly 1/16, 1/8, 1/4 or 1/2.
All inputs are finite; a program needn't handle non-finite values.
Results may differ from the reference program's by a relative error of at most 0.001.
Values may be sent and summed in bfloat16 or wider, within the bound.
No kernel may reach another device: no remote copies, remote signals or barrier semaphores. Data moves between devices by JAX's collectives and lax.ppermute only.
A program may use at most 32 MiB of HBM per device.

```python
import jax
import jax.numpy as jnp
from jax import lax

BS = 128
SA = 1
OUTS = 8
ORDER = 2
PANELS = 32
N_ROW = 32
N_COL = 32


def draw_targets(key, part):
    key_level, key_order, key_slot = jax.random.split(key, 3)
    powers = jax.random.randint(key_level, (N_ROW, N_COL), 0, 4)
    levels = jnp.left_shift(jnp.ones((N_ROW, N_COL), jnp.int32), powers)
    order_keys = jax.random.split(key_order, N_ROW * N_COL)

    def ranking(single_key):
        return jax.random.permutation(single_key, PANELS * SA)
    ranks = jax.vmap(ranking)(order_keys).reshape(N_ROW, N_COL, PANELS, SA)
    slots = jax.random.randint(key_slot, (N_ROW, N_COL, PANELS, SA), 0, OUTS)
    active = ranks % 16 < levels[:, :, None, None]
    return jnp.where(active, slots, OUTS).astype(jnp.int32)


def steps_of(rng, shape, shards, smallest, largest):
    factor_of = 1.0
    for dim, shards_of in shards:
        draws = jax.random.uniform(jax.random.fold_in(jax.random.fold_in(rng, 6), dim), (shards_of,), jnp.float32, smallest / len(shards), largest / len(shards))
        factor_of = factor_of * jnp.repeat(jnp.exp(draws), shape[dim] // shards_of).reshape((-1,) + (1,) * (len(shape) - 1 - dim))
    return factor_of


def gaussian(own_key, dims, width, most, cuts=(), kind=jnp.bfloat16):
    gain = steps_of(own_key, dims, cuts, -0.22, 0.18) if cuts else 1.0
    drawn = jax.random.normal(own_key, dims, jnp.float32) * width * gain
    return jnp.minimum(jnp.maximum(drawn, -most), most).astype(kind)


def setup_inputs(seed: int = 0) -> dict:
    seeds = jax.random.split(jax.random.key(seed), 5)
    return {
        "left_term": gaussian(seeds[0], (N_ROW, PANELS, SA, 2, BS, BS), 1.0, 6.0, ((0, 32), (1, 32))),
        "right_factor": gaussian(seeds[1], (PANELS, N_COL, BS, 2 * BS), 0.125, 0.75, ((0, 32), (1, 32))),
        "targets": draw_targets(jax.random.fold_in(seeds[4], 71), 0),
        "propagator_in": gaussian(seeds[3], (N_ROW, N_COL, OUTS, 2, BS, BS), 1.0, 6.0, ((0, 32), (1, 32)), jnp.float32),
    }


STEP_SIZE = 0.5


def reference(left_term, right_factor, targets, propagator_in):
    scaling = STEP_SIZE / ORDER

    def one_device(device_number):
        row_pos = device_number // N_COL
        col_pos = device_number % N_COL
        start_totals = jnp.zeros((OUTS, 2, BS, BS), jnp.float32)

        def one_task(task_number, totals):
            panel_pos = task_number // SA
            member = task_number % SA
            target_slot = targets[row_pos, col_pos, panel_pos, member]

            def add_product(current):
                pair_block = left_term[row_pos, panel_pos, member]
                matrix = right_factor[panel_pos, col_pos]
                from_real = jnp.dot(pair_block[0], matrix, preferred_element_type=jnp.float32)
                from_imag = jnp.dot(pair_block[1], matrix, preferred_element_type=jnp.float32)
                real_part = from_real[:, :BS] - from_imag[:, BS:]
                imag_part = from_real[:, BS:] + from_imag[:, :BS]
                update = jnp.stack([scaling * imag_part, -scaling * real_part], axis=0)
                return current.at[target_slot].add(update)

            def keep_same(current):
                return current

            return lax.cond(target_slot < OUTS, add_product, keep_same, totals)

        return lax.fori_loop(0, PANELS * SA, one_task, start_totals)

    numbers = jnp.arange(N_ROW * N_COL, dtype=jnp.int32)
    terms = lax.map(one_device, numbers).reshape(N_ROW, N_COL, OUTS, 2, BS, BS)
    return terms.astype(jnp.bfloat16), propagator_in + terms
```

```python
import jax
import jax.numpy as jnp
from jax import lax
from jax.experimental import pallas as pl
from jax.experimental.pallas import tpu as pltpu
from jax.sharding import PartitionSpec as P

ORDER = 2
STEP_SIZE = 0.5
SCALING = STEP_SIZE / ORDER
RUNS = 2
CLASSES = 4


def shifted(columns, step):
    length = columns // RUNS
    return [
        (run * length + place, run * length + (place + step) % length)
        for run in range(RUNS)
        for place in range(length)
    ]


def gather_left(pair, columns):
    length = columns // RUNS
    groups = [
        [run * length + member * CLASSES + start for member in range(length // CLASSES)]
        for run in range(RUNS)
        for start in range(CLASSES)
    ]
    own = lax.all_gather(pair, "col", axis_index_groups=groups)
    half = own.shape[0] // 2
    after = lax.ppermute(own, "col", shifted(columns, -1))
    before = lax.ppermute(own, "col", shifted(columns, 1))
    far_low = lax.ppermute(own[:half], "col", shifted(columns, 2))
    far_high = lax.ppermute(own[half:], "col", shifted(columns, -2))
    return own, after, far_low, far_high, before


def product_kernel(
    members, place_ref, targets_ref, own, after, far_low, far_high, before, right, base_ref,
    next_hbm, sum_hbm, totals, next_buf, sum_buf, next_sem, sum_sem,
):
    slots = totals.shape[0]
    edge = totals.shape[2]
    length = members * CLASSES
    start, my_run = place_ref[0], place_ref[1]
    totals[...] = jnp.zeros_like(totals)

    def add_class(ref, distance, first, count):
        residue = lax.rem(start + distance, CLASSES)

        def step(index, carry):
            member = first + index // RUNS
            flip = lax.rem(index, RUNS)
            run = lax.rem(my_run + flip, RUNS)
            panel = run * length + member * CLASSES + residue
            slot = targets_ref[panel]

            @pl.when(slot < slots)
            def _():
                product = jnp.dot(
                    ref[index // RUNS, flip], right[panel], preferred_element_type=jnp.float32
                )
                real = product[:edge, :edge] - product[edge:, edge:]
                imag = product[:edge, edge:] + product[edge:, :edge]
                totals[slot, 0] += imag
                totals[slot, 1] -= real

            return carry

        lax.fori_loop(0, count * RUNS, step, 0)

    add_class(own, 0, 0, members)
    add_class(after, 1, 0, members)
    add_class(far_low, 2, 0, members // 2)
    add_class(far_high, 2, members // 2, members // 2)
    add_class(before, 3, 0, members)

    def out_copies(slot):
        return (
            pltpu.make_async_copy(next_buf.at[slot], next_hbm.at[slot], next_sem.at[slot]),
            pltpu.make_async_copy(sum_buf.at[slot], sum_hbm.at[slot], sum_sem.at[slot]),
        )

    for slot in range(slots):
        term = totals[slot] * SCALING
        next_buf[slot] = term.astype(jnp.bfloat16)
        sum_buf[slot] = base_ref[slot] + term
        for copy in out_copies(slot):
            copy.start()
    for slot in range(slots):
        for copy in out_copies(slot):
            copy.wait()


def per_device(left_term, right_factor, targets, propagator_in):
    columns, rows = lax.axis_size("col"), lax.axis_size("row")
    edge = left_term.shape[4]
    slots = propagator_in.shape[2]
    length = columns // RUNS
    members = length // CLASSES
    mine = left_term.reshape(2 * edge, edge)
    other = lax.ppermute(
        mine, "col", [(c, (c + length) % columns) for c in range(columns)]
    )
    pair = jnp.stack([mine, other])
    copies = jnp.broadcast_to(right_factor[0, 0], (rows, edge, 2 * edge))
    pair, copies = lax.optimization_barrier((pair, copies))
    right = lax.all_to_all(copies, "row", 0, 0)
    own, after, far_low, far_high, before = gather_left(pair, columns)
    column = lax.axis_index("col")
    place = jnp.stack([column % CLASSES, column // length]).astype(jnp.int32)
    block = (slots, 2, edge, edge)
    in_vmem = pl.BlockSpec(memory_space=pltpu.VMEM)
    in_smem = pl.BlockSpec(memory_space=pltpu.SMEM)
    in_any = pl.BlockSpec(memory_space=pl.ANY)

    def kernel(*refs):
        product_kernel(members, *refs)

    next_term, total = pl.pallas_call(
        kernel,
        out_shape=(
            jax.ShapeDtypeStruct(block, jnp.bfloat16),
            jax.ShapeDtypeStruct(block, jnp.float32),
        ),
        in_specs=[in_smem, in_smem] + [in_vmem] * 7,
        out_specs=(in_any, in_any),
        scratch_shapes=[
            pltpu.VMEM(block, jnp.float32),
            pltpu.VMEM(block, jnp.bfloat16),
            pltpu.VMEM(block, jnp.float32),
            pltpu.SemaphoreType.DMA((slots,)),
            pltpu.SemaphoreType.DMA((slots,)),
        ],
        compiler_params=pltpu.CompilerParams(vmem_limit_bytes=24 * 1024 * 1024),
        cost_estimate=pl.CostEstimate(flops=300_000_000, bytes_accessed=7_000_000, transcendentals=0),
    )(
        place, targets[0, 0, :, 0], own, after, far_low, far_high, before, right,
        propagator_in.reshape(block),
    )
    shape = propagator_in.shape
    return next_term.reshape(shape), total.reshape(shape)


def solution(mesh):
    in_specs = (
        P("row", "col", None, None, None, None),
        P("row", "col", None, None),
        P("row", "col", None, None),
        P("row", "col", None, None, None, None),
    )
    out_specs = (P("row", "col", None, None, None, None), P("row", "col", None, None, None, None))
    return jax.shard_map(
        per_device, mesh=mesh, in_specs=in_specs, out_specs=out_specs, check_vma=False
    )
```

```python
import jax
import jax.numpy as jnp
from jax import lax
from jax.experimental import pallas as pl
from jax.experimental.pallas import tpu as pltpu
from jax.sharding import PartitionSpec as P

ORDER = 2
STEP_SIZE = 0.5
SCALING = STEP_SIZE / ORDER
RUNS = 2
CORES = 2
STRIDE = 4


def moved(value, columns, step):
    length = columns // RUNS
    pairs = [
        (run * length + place, run * length + (place + step) % length)
        for run in range(RUNS)
        for place in range(length)
    ]
    return lax.ppermute(value, "col", pairs)


def spread_kernel(block, copies, sems):
    moves = [pltpu.make_async_copy(block, copies.at[to], sems.at[to]) for to in range(copies.shape[0])]
    for move in moves:
        move.start()
    for move in moves:
        move.wait()


def add_panels(layout, length, meta, lefts, same_core, other_core, totals):
    slots, edge = totals.shape[0], totals.shape[2]
    panels = RUNS * length
    place, my_run, my_core = meta[panels], meta[panels + 1], meta[panels + 2]
    for ref, (delta, first) in zip(lefts, layout, strict=True):
        start = lax.rem(place + (delta + length), STRIDE)

        def step(index, carry, ref=ref, start=start, first=first):
            member, flip = index // RUNS, lax.rem(index, RUNS)
            run = lax.rem(my_run + flip, RUNS)
            panel = run * length + (first + member) * STRIDE + start
            slot = meta[panel]

            @pl.when(slot < slots)
            def _():
                at = panel // CORES
                block = jnp.where(panel % CORES == my_core, same_core[at], other_core[at])
                product = jnp.dot(ref[member, flip], block, preferred_element_type=jnp.float32)
                totals[slot, 0] += product[:edge, edge:] + product[edge:, :edge]
                totals[slot, 1] += product[edge:, edge:] - product[:edge, :edge]

            return carry

        lax.fori_loop(0, ref.shape[0] * RUNS, step, 0)


def first_kernel(layout, length, meta, *refs):
    *lefts, same_core, other_core, totals = refs
    totals[...] = jnp.zeros_like(totals)
    add_panels(layout, length, meta, lefts, same_core, other_core, totals)


def last_kernel(layout, length, meta, *refs):
    (*lefts, same_core, other_core, partial, base, next_hbm, sum_hbm,
     totals, next_buf, sum_buf, next_sem, sum_sem) = refs
    slots = totals.shape[0]
    totals[...] = partial[...]
    add_panels(layout, length, meta, lefts, same_core, other_core, totals)

    def out_copies(slot):
        return (
            pltpu.make_async_copy(next_buf.at[slot], next_hbm.at[slot], next_sem.at[slot]),
            pltpu.make_async_copy(sum_buf.at[slot], sum_hbm.at[slot], sum_sem.at[slot]),
        )

    for slot in range(slots):
        term = totals[slot] * SCALING
        next_buf[slot] = term.astype(jnp.bfloat16)
        sum_buf[slot] = base[slot] + term
        for copy in out_copies(slot):
            copy.start()
    for slot in range(slots):
        for copy in out_copies(slot):
            copy.wait()


def per_device(left_term, right_factor, targets, propagator_in):
    columns, rows = lax.axis_size("col"), lax.axis_size("row")
    edge = left_term.shape[4]
    slots = propagator_in.shape[2]
    length = columns // RUNS
    mine = left_term.reshape(2 * edge, edge)
    swap = [(c, (c + length) % columns) for c in range(columns)]

    other = lax.ppermute(mine, "col", swap)
    block = (slots, 2, edge, edge)
    in_vmem = pl.BlockSpec(memory_space=pltpu.VMEM)
    in_smem = pl.BlockSpec(memory_space=pltpu.SMEM)
    in_any = pl.BlockSpec(memory_space=pl.ANY)

    copies = pl.pallas_call(
        spread_kernel,
        out_shape=jax.ShapeDtypeStruct((rows // CORES, edge, 2 * edge), right_factor.dtype),
        in_specs=[in_vmem],
        out_specs=in_any,
        scratch_shapes=[pltpu.SemaphoreType.DMA((rows // CORES,))],
        cost_estimate=pl.CostEstimate(flops=0, bytes_accessed=8_000_000, transcendentals=0),
    )(right_factor[0, 0])
    column, row = lax.axis_index("col"), lax.axis_index("row")
    place = jnp.stack([column % length, column // length, row % CORES]).astype(jnp.int32)
    meta = jnp.concatenate([targets[0, 0, :, 0], place])
    other, copies, meta = lax.optimization_barrier((other, copies, meta))
    same_groups = [list(range(core, rows, CORES)) for core in range(CORES)]
    same_core = lax.all_to_all(copies, "row", 0, 0, axis_index_groups=same_groups)
    members = length // STRIDE
    groups = [
        [run * length + member * STRIDE + start for member in range(members)]
        for run in range(RUNS)
        for start in range(STRIDE)
    ]
    both = lax.all_gather(jnp.stack([mine, other]), "col", axis_index_groups=groups)
    low, high = both[: members // 2], both[members // 2 :]
    before, after2 = moved(low, columns, 1), moved(high, columns, -1)
    before2, after = moved(high, columns, 1), moved(low, columns, -1)
    far, far2 = moved(before, columns, 1), moved(after2, columns, -1)
    across = [(r, r ^ 1) for r in range(rows)]
    tied, _ = lax.optimization_barrier((same_core, both))
    other_core = lax.ppermute(tied, "row", across)
    half = members // 2
    early = [(both, (0, 0)), (before, (-1, 0)), (after2, (1, half)), (after, (1, 0)), (before2, (-1, half))]
    late = [(far, (-2, 0)), (far2, (2, half))]

    def first(*refs):
        first_kernel([g[1] for g in early], length, *refs)

    def last(*refs):
        last_kernel([g[1] for g in late], length, *refs)

    partial = pl.pallas_call(
        first,
        out_shape=jax.ShapeDtypeStruct(block, jnp.float32),
        in_specs=[in_smem] + [in_vmem] * (len(early) + 2),
        out_specs=in_vmem,
        compiler_params=pltpu.CompilerParams(vmem_limit_bytes=20 * 1024 * 1024),
        cost_estimate=pl.CostEstimate(flops=200_000_000, bytes_accessed=4_000_000, transcendentals=0),
    )(meta, *[g[0] for g in early], same_core, other_core)
    next_term, total = pl.pallas_call(
        last,
        out_shape=(
            jax.ShapeDtypeStruct(block, jnp.bfloat16),
            jax.ShapeDtypeStruct(block, jnp.float32),
        ),
        in_specs=[in_smem] + [in_vmem] * (len(late) + 4),
        out_specs=(in_any, in_any),
        scratch_shapes=[
            pltpu.VMEM(block, jnp.float32),
            pltpu.VMEM(block, jnp.bfloat16),
            pltpu.VMEM(block, jnp.float32),
            pltpu.SemaphoreType.DMA((slots,)),
            pltpu.SemaphoreType.DMA((slots,)),
        ],
        compiler_params=pltpu.CompilerParams(vmem_limit_bytes=20 * 1024 * 1024),
        cost_estimate=pl.CostEstimate(flops=100_000_000, bytes_accessed=4_000_000, transcendentals=0),
    )(meta, *[g[0] for g in late], same_core, other_core, partial, propagator_in.reshape(block))
    shape = propagator_in.shape
    return next_term.reshape(shape), total.reshape(shape)


def solution(mesh):
    in_specs = (
        P("row", "col", None, None, None, None),
        P("row", "col", None, None),
        P("row", "col", None, None),
        P("row", "col", None, None, None, None),
    )
    out_specs = (P("row", "col", None, None, None, None), P("row", "col", None, None, None, None))
    return jax.shard_map(
        per_device, mesh=mesh, in_specs=in_specs, out_specs=out_specs, check_vma=False
    )
```

```python
import jax
import jax.numpy as jnp
from jax import lax
from jax.experimental import pallas as pl
from jax.experimental.pallas import tpu as pltpu
from jax.sharding import PartitionSpec as P

ORDER = 2
STEP_SIZE = 0.5
SCALING = STEP_SIZE / ORDER
RUNS = 2
CORES = 2
STRIDE = 4


def moved(value, columns, step):
    length = columns // RUNS
    pairs = [
        (run * length + place, run * length + (place + step) % length)
        for run in range(RUNS)
        for place in range(length)
    ]
    return lax.ppermute(value, "col", pairs)


def spread_kernel(block, copies, sems):
    moves = [pltpu.make_async_copy(block, copies.at[to], sems.at[to]) for to in range(copies.shape[0])]
    for move in moves:
        move.start()
    for move in moves:
        move.wait()


def add_panels(layout, length, meta, lefts, same_core, other_core, totals, touched=None):
    slots, edge = totals.shape[0], totals.shape[2]
    panels = RUNS * length
    place, my_run, my_core = meta[panels], meta[panels + 1], meta[panels + 2]
    for ref, (delta, first) in zip(lefts, layout, strict=True):
        start = lax.rem(place + (delta + length), STRIDE)

        def step(index, carry, ref=ref, start=start, first=first):
            member, flip = index // RUNS, lax.rem(index, RUNS)
            run = lax.rem(my_run + flip, RUNS)
            panel = run * length + (first + member) * STRIDE + start
            slot = meta[panel]

            @pl.when(slot < slots)
            def _():
                at = panel // CORES
                block = jnp.where(panel % CORES == my_core, same_core[at], other_core[at])
                product = jnp.dot(ref[member, flip], block, preferred_element_type=jnp.float32)
                totals[slot, 0] += product[:edge, edge:] + product[edge:, :edge]
                totals[slot, 1] += product[edge:, edge:] - product[:edge, :edge]
                if touched is not None:
                    touched[slot] = 1

            return carry

        lax.fori_loop(0, ref.shape[0] * RUNS, step, 0)


def out_copies(slot, next_buf, sum_buf, next_hbm, sum_hbm, next_sem, sum_sem):
    return (
        pltpu.make_async_copy(next_buf.at[slot], next_hbm.at[slot], next_sem.at[slot]),
        pltpu.make_async_copy(sum_buf.at[slot], sum_hbm.at[slot], sum_sem.at[slot]),
    )


def write_slot(slot, totals, base, next_buf, sum_buf):
    term = totals[slot] * SCALING
    next_buf[slot] = term.astype(jnp.bfloat16)
    sum_buf[slot] = base[slot] + term


def first_kernel(layout, length, meta, *refs):
    (*lefts, same_core, other_core, base, totals, next_hbm, sum_hbm,
     next_buf, sum_buf, next_sem, sum_sem) = refs
    slots = totals.shape[0]
    totals[...] = jnp.zeros_like(totals)
    add_panels(layout, length, meta, lefts, same_core, other_core, totals)
    for slot in range(slots):
        write_slot(slot, totals, base, next_buf, sum_buf)
        for copy in out_copies(slot, next_buf, sum_buf, next_hbm, sum_hbm, next_sem, sum_sem):
            copy.start()
    for slot in range(slots):
        for copy in out_copies(slot, next_buf, sum_buf, next_hbm, sum_hbm, next_sem, sum_sem):
            copy.wait()


def last_kernel(layout, length, meta, *refs):
    (*lefts, same_core, other_core, base, _, _, _, totals, next_hbm, sum_hbm,
     touched, next_buf, sum_buf, next_sem, sum_sem) = refs
    slots = totals.shape[0]
    for slot in range(slots):
        touched[slot] = 0
    add_panels(layout, length, meta, lefts, same_core, other_core, totals, touched)
    for slot in range(slots):

        @pl.when(touched[slot] == 1)
        def _():
            write_slot(slot, totals, base, next_buf, sum_buf)
            for copy in out_copies(slot, next_buf, sum_buf, next_hbm, sum_hbm, next_sem, sum_sem):
                copy.start()

    for slot in range(slots):

        @pl.when(touched[slot] == 1)
        def _():
            for copy in out_copies(slot, next_buf, sum_buf, next_hbm, sum_hbm, next_sem, sum_sem):
                copy.wait()


def per_device(left_term, right_factor, targets, propagator_in):
    columns, rows = lax.axis_size("col"), lax.axis_size("row")
    edge = left_term.shape[4]
    slots = propagator_in.shape[2]
    length = columns // RUNS
    mine = left_term.reshape(2 * edge, edge)
    swap = [(c, (c + length) % columns) for c in range(columns)]

    other = lax.ppermute(mine, "col", swap)
    block = (slots, 2, edge, edge)
    in_vmem = pl.BlockSpec(memory_space=pltpu.VMEM)
    in_smem = pl.BlockSpec(memory_space=pltpu.SMEM)
    in_any = pl.BlockSpec(memory_space=pl.ANY)

    copies = pl.pallas_call(
        spread_kernel,
        out_shape=jax.ShapeDtypeStruct((rows // CORES, edge, 2 * edge), right_factor.dtype),
        in_specs=[in_vmem],
        out_specs=in_any,
        scratch_shapes=[pltpu.SemaphoreType.DMA((rows // CORES,))],
        cost_estimate=pl.CostEstimate(flops=0, bytes_accessed=1_114_112, transcendentals=0),
    )(right_factor[0, 0])
    column, row = lax.axis_index("col"), lax.axis_index("row")
    place = jnp.stack([column % length, column // length, row % CORES]).astype(jnp.int32)
    meta = jnp.concatenate([targets[0, 0, :, 0], place])
    other, copies, meta = lax.optimization_barrier((other, copies, meta))
    same_groups = [list(range(core, rows, CORES)) for core in range(CORES)]
    same_core = lax.all_to_all(copies, "row", 0, 0, axis_index_groups=same_groups)
    members = length // STRIDE
    groups = [
        [run * length + member * STRIDE + start for member in range(members)]
        for run in range(RUNS)
        for start in range(STRIDE)
    ]
    both = lax.all_gather(jnp.stack([mine, other]), "col", axis_index_groups=groups)
    low, high = both[: members // 2], both[members // 2 :]
    before, after2 = moved(low, columns, 1), moved(high, columns, -1)
    before2, after = moved(high, columns, 1), moved(low, columns, -1)
    far, far2 = moved(before, columns, 1), moved(after2, columns, -1)
    across = [(r, r ^ 1) for r in range(rows)]
    tied, _ = lax.optimization_barrier((same_core, both))
    other_core = lax.ppermute(tied, "row", across)
    half = members // 2
    early = [(both, (0, 0)), (before, (-1, 0)), (after2, (1, half)), (after, (1, 0)), (before2, (-1, half))]
    late = [(far, (-2, 0)), (far2, (2, half))]

    def first(*refs):
        first_kernel([g[1] for g in early], length, *refs)

    def last(*refs):
        last_kernel([g[1] for g in late], length, *refs)

    base = propagator_in.reshape(block)
    out_shape = (
        jax.ShapeDtypeStruct(block, jnp.float32),
        jax.ShapeDtypeStruct(block, jnp.bfloat16),
        jax.ShapeDtypeStruct(block, jnp.float32),
    )
    buffers = [
        pltpu.VMEM(block, jnp.bfloat16),
        pltpu.VMEM(block, jnp.float32),
        pltpu.SemaphoreType.DMA((slots,)),
        pltpu.SemaphoreType.DMA((slots,)),
    ]
    partial, next_term, total = pl.pallas_call(
        first,
        out_shape=out_shape,
        in_specs=[in_smem] + [in_vmem] * (len(early) + 3),
        out_specs=(in_vmem, in_any, in_any),
        scratch_shapes=buffers,
        compiler_params=pltpu.CompilerParams(vmem_limit_bytes=20 * 1024 * 1024),
        cost_estimate=pl.CostEstimate(flops=200_000_000, bytes_accessed=4_000_000, transcendentals=0),
    )(meta, *[g[0] for g in early], same_core, other_core, base)
    _, next_term, total = pl.pallas_call(
        last,
        out_shape=out_shape,
        in_specs=[in_smem] + [in_vmem] * (len(late) + 4) + [in_any, in_any],
        out_specs=(in_vmem, in_any, in_any),
        scratch_shapes=[pltpu.SMEM((slots,), jnp.int32)] + buffers,
        input_output_aliases={len(late) + 4 + i: i for i in range(3)},
        compiler_params=pltpu.CompilerParams(vmem_limit_bytes=20 * 1024 * 1024),
        cost_estimate=pl.CostEstimate(flops=70_000_000, bytes_accessed=2_000_000, transcendentals=0),
    )(meta, *[g[0] for g in late], same_core, other_core, base, partial, next_term, total)
    shape = propagator_in.shape
    return next_term.reshape(shape), total.reshape(shape)


def solution(mesh):
    in_specs = (
        P("row", "col", None, None, None, None),
        P("row", "col", None, None),
        P("row", "col", None, None),
        P("row", "col", None, None, None, None),
    )
    out_specs = (P("row", "col", None, None, None, None), P("row", "col", None, None, None, None))
    return jax.shard_map(
        per_device, mesh=mesh, in_specs=in_specs, out_specs=out_specs, check_vma=False
    )
```

```python
import jax
import jax.numpy as jnp
from jax import lax
from jax.experimental import pallas as pl
from jax.experimental.pallas import tpu as pltpu
from jax.sharding import PartitionSpec as P

ORDER = 2
STEP_SIZE = 0.5
SCALING = STEP_SIZE / ORDER
RUNS = 2
CORES = 2
STRIDE = 4


def moved(value, columns, step):
    length = columns // RUNS
    pairs = [
        (run * length + place, run * length + (place + step) % length)
        for run in range(RUNS)
        for place in range(length)
    ]
    return lax.ppermute(value, "col", pairs)


def spread_kernel(block, copies, sems):
    moves = [pltpu.make_async_copy(block, copies.at[to], sems.at[to]) for to in range(copies.shape[0])]
    for move in moves:
        move.start()
    for move in moves:
        move.wait()


def add_panels(layout, length, meta, lefts, same_core, other_core, totals, touched=None):
    slots, edge = totals.shape[0], totals.shape[2]
    panels = RUNS * length
    place, my_run, my_core = meta[panels], meta[panels + 1], meta[panels + 2]
    for ref, (delta, first) in zip(lefts, layout, strict=True):
        start = lax.rem(place + (delta + length), STRIDE)

        def step(index, carry, ref=ref, start=start, first=first):
            member, flip = index // RUNS, lax.rem(index, RUNS)
            run = lax.rem(my_run + flip, RUNS)
            panel = run * length + (first + member) * STRIDE + start
            slot = meta[panel]

            @pl.when(slot < slots)
            def _():
                at = panel // CORES
                block = jnp.where(panel % CORES == my_core, same_core[at], other_core[at])
                product = jnp.dot(ref[member, flip], block, preferred_element_type=jnp.float32)
                totals[slot, 0] += product[:edge, edge:] + product[edge:, :edge]
                totals[slot, 1] += product[edge:, edge:] - product[:edge, :edge]
                if touched is not None:
                    touched[slot] = 1

            return carry

        lax.fori_loop(0, ref.shape[0] * RUNS, step, 0)


def out_copies(slot, next_buf, sum_buf, next_hbm, sum_hbm, next_sem, sum_sem):
    return (
        pltpu.make_async_copy(next_buf.at[slot], next_hbm.at[slot], next_sem.at[slot]),
        pltpu.make_async_copy(sum_buf.at[slot], sum_hbm.at[slot], sum_sem.at[slot]),
    )


def write_slot(slot, totals, base, next_buf, sum_buf):
    term = totals[slot] * SCALING
    next_buf[slot] = term.astype(jnp.bfloat16)
    sum_buf[slot] = base[slot] + term


def first_kernel(layout, length, meta, *refs):
    (*lefts, same_core, other_core, base, totals, next_hbm, sum_hbm,
     next_buf, sum_buf, next_sem, sum_sem) = refs
    slots = totals.shape[0]
    totals[...] = jnp.zeros_like(totals)
    add_panels(layout, length, meta, lefts, same_core, other_core, totals)
    for slot in range(slots):
        write_slot(slot, totals, base, next_buf, sum_buf)
        for copy in out_copies(slot, next_buf, sum_buf, next_hbm, sum_hbm, next_sem, sum_sem):
            copy.start()
    for slot in range(slots):
        for copy in out_copies(slot, next_buf, sum_buf, next_hbm, sum_hbm, next_sem, sum_sem):
            copy.wait()


def last_kernel(layout, length, meta, *refs):
    (*lefts, same_core, other_core, base, _, _, _, totals, next_hbm, sum_hbm,
     touched, next_buf, sum_buf, next_sem, sum_sem) = refs
    slots = totals.shape[0]
    for slot in range(slots):
        touched[slot] = 0
    add_panels(layout, length, meta, lefts, same_core, other_core, totals, touched)
    for slot in range(slots):

        @pl.when(touched[slot] == 1)
        def _():
            write_slot(slot, totals, base, next_buf, sum_buf)
            for copy in out_copies(slot, next_buf, sum_buf, next_hbm, sum_hbm, next_sem, sum_sem):
                copy.start()

    for slot in range(slots):

        @pl.when(touched[slot] == 1)
        def _():
            for copy in out_copies(slot, next_buf, sum_buf, next_hbm, sum_hbm, next_sem, sum_sem):
                copy.wait()


def per_device(left_term, right_factor, targets, propagator_in):
    columns, rows = lax.axis_size("col"), lax.axis_size("row")
    edge = left_term.shape[4]
    slots = propagator_in.shape[2]
    length = columns // RUNS
    mine = left_term.reshape(2 * edge, edge)
    swap = [(c, (c + length) % columns) for c in range(columns)]

    other = lax.ppermute(mine, "col", swap)
    block = (slots, 2, edge, edge)
    in_vmem = pl.BlockSpec(memory_space=pltpu.VMEM)
    in_smem = pl.BlockSpec(memory_space=pltpu.SMEM)
    in_any = pl.BlockSpec(memory_space=pl.ANY)

    copies = pl.pallas_call(
        spread_kernel,
        out_shape=jax.ShapeDtypeStruct((rows // CORES, edge, 2 * edge), right_factor.dtype),
        in_specs=[in_vmem],
        out_specs=in_vmem,
        scratch_shapes=[pltpu.SemaphoreType.DMA((rows // CORES,))],
        cost_estimate=pl.CostEstimate(flops=0, bytes_accessed=1_114_112, transcendentals=0),
    )(right_factor[0, 0])
    column, row = lax.axis_index("col"), lax.axis_index("row")
    place = jnp.stack([column % length, column // length, row % CORES]).astype(jnp.int32)
    meta = jnp.concatenate([targets[0, 0, :, 0], place])
    other, copies, meta = lax.optimization_barrier((other, copies, meta))
    same_groups = [list(range(core, rows, CORES)) for core in range(CORES)]
    same_core = lax.all_to_all(copies, "row", 0, 0, axis_index_groups=same_groups)
    members = length // STRIDE
    groups = [
        [run * length + member * STRIDE + start for member in range(members)]
        for run in range(RUNS)
        for start in range(STRIDE)
    ]
    both = lax.all_gather(jnp.stack([mine, other]), "col", axis_index_groups=groups)
    low, high = both[: members // 2], both[members // 2 :]
    before, after2 = moved(low, columns, 1), moved(high, columns, -1)
    before2, after = moved(high, columns, 1), moved(low, columns, -1)
    far, far2 = moved(before, columns, 1), moved(after2, columns, -1)
    across = [(r, r ^ 1) for r in range(rows)]
    tied, _ = lax.optimization_barrier((same_core, both))
    other_core = lax.ppermute(tied, "row", across)
    half = members // 2
    early = [(both, (0, 0)), (before, (-1, 0)), (after2, (1, half)), (after, (1, 0)), (before2, (-1, half))]
    late = [(far, (-2, 0)), (far2, (2, half))]

    def first(*refs):
        first_kernel([g[1] for g in early], length, *refs)

    def last(*refs):
        last_kernel([g[1] for g in late], length, *refs)

    base = propagator_in.reshape(block)
    out_shape = (
        jax.ShapeDtypeStruct(block, jnp.float32),
        jax.ShapeDtypeStruct(block, jnp.bfloat16),
        jax.ShapeDtypeStruct(block, jnp.float32),
    )
    buffers = [
        pltpu.VMEM(block, jnp.bfloat16),
        pltpu.VMEM(block, jnp.float32),
        pltpu.SemaphoreType.DMA((slots,)),
        pltpu.SemaphoreType.DMA((slots,)),
    ]
    partial, next_term, total = pl.pallas_call(
        first,
        out_shape=out_shape,
        in_specs=[in_smem] + [in_vmem] * (len(early) + 3),
        out_specs=(in_vmem, in_any, in_any),
        scratch_shapes=buffers,
        compiler_params=pltpu.CompilerParams(vmem_limit_bytes=20 * 1024 * 1024),
        cost_estimate=pl.CostEstimate(flops=200_000_000, bytes_accessed=4_000_000, transcendentals=0),
    )(meta, *[g[0] for g in early], same_core, other_core, base)
    _, next_term, total = pl.pallas_call(
        last,
        out_shape=out_shape,
        in_specs=[in_smem] + [in_vmem] * (len(late) + 4) + [in_any, in_any],
        out_specs=(in_vmem, in_any, in_any),
        scratch_shapes=[pltpu.SMEM((slots,), jnp.int32)] + buffers,
        input_output_aliases={len(late) + 4 + i: i for i in range(3)},
        compiler_params=pltpu.CompilerParams(vmem_limit_bytes=20 * 1024 * 1024),
        cost_estimate=pl.CostEstimate(flops=70_000_000, bytes_accessed=2_000_000, transcendentals=0),
    )(meta, *[g[0] for g in late], same_core, other_core, base, partial, next_term, total)
    shape = propagator_in.shape
    return next_term.reshape(shape), total.reshape(shape)


def solution(mesh):
    in_specs = (
        P("row", "col", None, None, None, None),
        P("row", "col", None, None),
        P("row", "col", None, None),
        P("row", "col", None, None, None, None),
    )
    out_specs = (P("row", "col", None, None, None, None), P("row", "col", None, None, None, None))
    return jax.shard_map(
        per_device, mesh=mesh, in_specs=in_specs, out_specs=out_specs, check_vma=False
    )
```
